32 devices in a mesh: groups: 2 (over y), virt: 4 (over z), occ: 2 (over x), rep: 2 (over core).
Axes of the slice: x: 2, y: 2, z: 4, core: 2. Of those that a mesh axis runs over, the one named last changes fastest.
Arguments:
- amplitudes: bfloat16 [4096, 1024], P(('groups', 'occ'), 'virt'), parts along dimension 0, may hold values from -6 to 6
- live_mask: int32 [128, 8], P(('groups', 'occ'), 'virt'), parts along dimension 0, may hold values 0 or 1
- integrals: bfloat16 [16, 4, 128, 128], P(('groups', 'virt'), 'rep'), parts along dimension 0, may hold values from -0.25 to 0.25
- coupled_tiles: int32 [16, 4], P(('groups', 'virt'), 'rep'), parts along dimension 0, may hold values from 0 to 7, all different within a row
Outputs:
- residual: bfloat16 [4096, 1024], P(('groups', 'occ'), ('virt', 'rep')), parts along dimension 0
The draws below stay inside these ranges and needn't reach their ends.
There are 2 independent parts, one for each index of `groups`. The reference program is written for one: setup_inputs(seed, part) draws one part's arguments, and reference() takes and returns one part's arrays. A program takes and returns all parts, laid end to end along the dimension named above; each array names one. Nothing has to cross between parts.
Inputs may be any that keep to these rules, and one draw needn't show every extreme that they name: `coupled_tiles`: each row names 4 different tiles.
All inputs are finite; a program needn't handle non-finite values. No bound on the sum of `live_mask` on one device may be relied on, other than what follows from the above.
Results may differ from the reference program's by a relative error of at most 0.001.
Values may be sent and summed in bfloat16 or wider, within the bound.
A program may use at most 128 MiB of HBM per device.

```python
import jax
import jax.numpy as jnp
from jax import lax

W = 128
RB = 32
NT = 8
KV = 4
OP = 2048


def place_ends(values, stream_key, low, high):
    dims = values.shape
    place = [jax.random.randint(jax.random.fold_in(stream_key, axis), (), 0, dims[axis]) for axis in range(len(dims))]
    values = values.at[tuple(place)].set(low)
    longest = dims.index(max(dims))
    place[longest] = (place[longest] + 1) % dims[longest]
    return values.at[tuple(place)].set(high)


def shard_levels(rng, extent, pieces, smallest, top_value):
    loudness = 1.0
    for dim, parts in pieces:
        steps = jax.random.uniform(jax.random.fold_in(jax.random.fold_in(rng, 6), dim), (parts,), jnp.float32, smallest / len(pieces), top_value / len(pieces))
        loudness = loudness * jnp.repeat(jnp.exp(steps), extent[dim] // parts).reshape((-1,) + (1,) * (len(extent) - 1 - dim))
    return loudness


def different_ones(own_key, rows, count, top, lift):
    order = jax.random.permutation(jax.random.fold_in(own_key, 1), count)
    boost = order
    for power in range(3):
        boost = boost * boost // count
    boost = boost * lift // count
    tickets = jax.random.randint(jax.random.fold_in(own_key, 2), (rows, count), 0, 4096) + boost
    holders = jax.random.permutation(jax.random.fold_in(own_key, 3), rows)[jnp.arange(count) % rows]
    tickets = jnp.where(jnp.arange(rows)[:, None] == holders[None, :], 1 << 14, tickets)
    priority = tickets * count + jnp.arange(count)
    return lax.top_k(priority.astype(jnp.int32), top)[1].astype(jnp.int32)


def centred(own_key, shape, scale, most, split=(), held_as=jnp.bfloat16):
    result = scale * jax.random.normal(own_key, shape, jnp.float32)
    if split:
        result = result * shard_levels(own_key, shape, split, -0.22, 0.18)
    return jnp.clip(result, -most, most).astype(held_as)


def setup_inputs(seed: int = 0, part: int = 0) -> dict:
    arg_keys = jax.random.split(jax.random.key(seed), 5)
    own_keys = jax.random.split(jax.random.fold_in(arg_keys[4], part), 5)
    return {
        "amplitudes": centred(own_keys[0], (OP, NT * W), 1.0, 6.0, ((0, 2), (1, 4))),
        "live_mask": place_ends((jax.random.randint(own_keys[1], (OP // RB, NT), 0, 4) < 3).astype(jnp.int32), jax.random.fold_in(own_keys[1], 1), 0, 1),
        "integrals": centred(own_keys[2], (NT, KV, W, W), (KV * W) ** -0.5, 0.25, ((0, 4), (1, 2))),
        "coupled_tiles": different_ones(own_keys[3], NT, NT, KV, 8192),
    }


def reference(amplitudes, live_mask, integrals, coupled_tiles):
    row_total = amplitudes.shape[0]
    expanded = jnp.repeat(live_mask, RB, axis=0).astype(amplitudes.dtype)
    masked = amplitudes.reshape(row_total, NT, W) * expanded[:, :, None]

    def one_tile(operands):
        panel, chosen = operands
        picked = jnp.take(masked, chosen.astype(jnp.int32), axis=1).reshape(row_total, KV * W)
        return jnp.dot(picked, panel.reshape(KV * W, W), preferred_element_type=jnp.float32)

    columns = lax.map(one_tile, (integrals, coupled_tiles))
    return jnp.transpose(columns, (1, 0, 2)).reshape(row_total, NT * W).astype(jnp.bfloat16)
```

```python
import functools

import jax
import jax.numpy as jnp
from jax import lax
from jax.experimental import pallas as pl
from jax.experimental.pallas import tpu as pltpu
from jax.sharding import PartitionSpec as P

MESH = pl.DeviceIdType.MESH
CHUNKS = 4


def ladder_kernel(
    amps, live, ints, pattern, out,
    held, panels, codes, codes_s, dense, staged,
    load_sem, send_r, send_l, recv_sem,
    pan_load, pan_recv, pan_send, code_load, code_recv, code_send, code_copy,
    own_sem, mate_sem, back_sem, out_recv,
):
    count = lax.axis_size("virt")
    cores = lax.axis_size("rep")
    z = lax.axis_index("virt")
    r = lax.axis_index("rep")
    mate = 1 - r
    last = count - 1
    tiles, ks, width, _ = ints.shape
    half = held.shape[1]
    rows = half // CHUNKS
    block = amps.shape[0] // live.shape[0]
    is_end = jnp.logical_or(z == 0, z == last)
    works = jnp.logical_not(is_end)
    helps = jnp.logical_or(z == 1, z == last - 1)
    helper = jnp.where(z == 0, 1, last - 1)
    helped = jnp.where(z == 1, 0, last)

    barrier = pltpu.get_barrier_semaphore()
    pl.semaphore_signal(barrier, inc=1, device_id={"rep": mate}, device_id_type=MESH)

    @pl.when(z > 0)
    def _():
        for c in range(cores):
            pl.semaphore_signal(barrier, inc=1, device_id={"virt": z - 1, "rep": c}, device_id_type=MESH)

    @pl.when(z < last)
    def _():
        for c in range(cores):
            pl.semaphore_signal(barrier, inc=1, device_id={"virt": z + 1, "rep": c}, device_id_type=MESH)

    def part(c):
        return pl.ds(pl.multiple_of(c * rows, rows), rows)

    def load(c):
        start = pl.multiple_of(r * half + c * rows, rows)
        return pltpu.make_async_copy(amps.at[pl.ds(start, rows)], held.at[z, part(c)], load_sem.at[c])

    for c in range(CHUNKS):
        load(c).start()
    pan_in = pltpu.make_async_copy(ints, panels.at[0, r], pan_load)
    code_in = pltpu.make_async_copy(pattern, codes.at[0, r], code_load)
    pan_in.start()
    code_in.start()

    def remote(src, dst, send, recv, **where):
        return pltpu.make_async_remote_copy(
            src_ref=src, dst_ref=dst, send_sem=send, recv_sem=recv, device_id=where, device_id_type=MESH
        )

    pan_mate = remote(panels.at[0, r], panels.at[0, r], pan_send.at[0], pan_recv.at[0], rep=mate)
    code_mate = remote(codes.at[0, r], codes.at[0, r], code_send.at[0], code_recv.at[0], rep=mate)
    pan_help = remote(panels.at[0, r], panels.at[1, r], pan_send.at[1], pan_recv.at[1], virt=helper)
    code_help = remote(codes.at[0, r], codes.at[1, r], code_send.at[1], code_recv.at[1], virt=helper)
    pan_pass = remote(panels.at[1, r], panels.at[1, r], pan_send.at[2], pan_recv.at[2], rep=mate)
    code_pass = remote(codes.at[1, r], codes.at[1, r], code_send.at[2], code_recv.at[2], rep=mate)

    def to_right(j, c):
        return remote(held.at[j, part(c)], held.at[j, part(c)], send_r.at[j, c], recv_sem.at[j, c], virt=z + 1)

    def to_left(j, c):
        return remote(held.at[j, part(c)], held.at[j, part(c)], send_l.at[j, c], recv_sem.at[j, c], virt=z - 1)

    goes_right = z + 1 <= last - 1
    goes_left = z - 1 >= 1

    pl.semaphore_wait(barrier, 1 + cores * ((z > 0).astype(jnp.int32) + (z < last).astype(jnp.int32)))

    pan_in.wait()
    code_in.wait()

    @pl.when(is_end)
    def _():
        pan_help.start()
        code_help.start()

    def mask(c):
        def one(b, _):
            at = pl.multiple_of(c * rows + b * block, block)
            which = (r * half + c * rows) // block + b
            for t in range(tiles):
                keep = live[which, t].astype(jnp.float32)
                keep = jnp.full((block, width), keep, jnp.float32).astype(held.dtype)
                view = held.at[z, pl.ds(at, block), pl.ds(t * width, width)]
                view[...] = view[...] * keep
            return 0

        lax.fori_loop(0, rows // block, one, 0, unroll=rows // block <= 8)

    for c in range(CHUNKS):
        load(c).wait()
        mask(c)

        @pl.when(goes_right)
        def _():
            to_right(z, c).start()

        @pl.when(goes_left)
        def _():
            to_left(z, c).start()

        if c == 0:
            @pl.when(works)
            def _():
                pan_mate.start()
                code_mate.start()

    def build(g):
        copy = pltpu.make_async_copy(codes.at[g], codes_s.at[g], code_copy)
        copy.start()
        copy.wait()

        def one(j, _):
            for t in range(tiles):
                for i in range(tiles):
                    total = jnp.zeros((width, width), dense.dtype)
                    for c in range(cores):
                        for k in range(ks):
                            hit = (codes_s[g, c, i, k] == j * tiles + t).astype(jnp.float32)
                            hit = jnp.full((width, width), hit, jnp.float32).astype(dense.dtype)
                            total = total + hit * panels[g, c, i, k]
                    dense[g, j, pl.ds(t * width, width), pl.ds(i * width, width)] = total
            return 0

        lax.fori_loop(0, count, one, 0)

    def arrive(j, c):
        to_right(j, c).wait_recv()

    def forward(c):
        def one(d, _):
            left, right = z - d, z + d

            @pl.when(jnp.logical_and(left >= 0, goes_right))
            def _():
                arrive(left, c)
                to_right(left, c).start()

            @pl.when(jnp.logical_and(right <= last, goes_left))
            def _():
                arrive(right, c)
                to_left(right, c).start()

            return 0

        lax.fori_loop(1, count, one, 0)

    def settle(c):
        def one(d, _):
            left, right = z - d, z + d

            @pl.when(jnp.logical_and(left >= 0, jnp.logical_not(goes_right)))
            def _():
                arrive(left, c)

            @pl.when(jnp.logical_and(right <= last, jnp.logical_not(goes_left)))
            def _():
                arrive(right, c)

            return 0

        lax.fori_loop(1, count, one, 0)

    def spot(owner, c):
        return pl.ds(pl.multiple_of(owner * half + c * rows, rows), rows)

    def own_out(c):
        return pltpu.make_async_copy(staged.at[0, r, part(c)], out.at[spot(r, c)], own_sem.at[c])

    def mate_out(c):
        return remote(
            staged.at[0, mate, part(c)], out.at[spot(r, c)], mate_sem.at[c], out_recv.at[r, c], rep=mate
        )

    def back_out(core, c):
        return remote(
            staged.at[1, core, part(c)], out.at[spot(r, c)], back_sem.at[core, c], out_recv.at[r, c],
            virt=helped, rep=core,
        )

    step = min(rows, 128)

    def multiply(g, c):
        def one(s, _):
            at = pl.ds(pl.multiple_of(c * rows + s * step, step), step)
            total = jnp.zeros((step, tiles * width), jnp.float32)
            for j in range(count):
                total = total + jnp.dot(held[j, at], dense[g, j], preferred_element_type=jnp.float32)
            for i in range(tiles):
                staged[g, i, at] = total[:, i * width : (i + 1) * width].astype(staged.dtype)
            return 0

        lax.fori_loop(0, rows // step, one, 0)

    @pl.when(works)
    def _():
        pan_mate.wait_recv()
        code_mate.wait_recv()
        build(0)

    @pl.when(helps)
    def _():
        pan_help.wait_recv()
        code_help.wait_recv()
        pan_pass.start()
        code_pass.start()

    @pl.when(works)
    def _():
        forward(0)

    @pl.when(helps)
    def _():
        pan_pass.wait_recv()
        code_pass.wait_recv()
        build(1)

    @pl.when(works)
    def _():
        for c in range(CHUNKS):
            if c + 1 < CHUNKS:
                forward(c + 1)
            settle(c)

            @pl.when(helps)
            def _():
                multiply(1, c)
                for core in range(cores):
                    back_out(core, c).start()

            multiply(0, c)
            mate_out(c).start()
            own_out(c).start()

    @pl.when(is_end)
    def _():
        pan_help.wait_send()
        code_help.wait_send()
        for c in range(CHUNKS):
            for core in range(cores):
                remote(
                    staged.at[0, 0, part(c)], out.at[spot(core, c)], mate_sem.at[c], out_recv.at[core, c], rep=mate
                ).wait_recv()

    for c in range(CHUNKS):
        @pl.when(goes_right)
        def _():
            to_right(z, c).wait_send()

        @pl.when(goes_left)
        def _():
            to_left(z, c).wait_send()

    @pl.when(works)
    def _():
        pan_mate.wait_send()
        code_mate.wait_send()
        for c in range(CHUNKS):
            def one(d, _):
                left, right = z - d, z + d

                @pl.when(jnp.logical_and(left >= 0, goes_right))
                def _():
                    to_right(left, c).wait_send()

                @pl.when(jnp.logical_and(right <= last, goes_left))
                def _():
                    to_left(right, c).wait_send()

                return 0

            lax.fori_loop(1, count, one, 0)
            own_out(c).wait()
            mate_out(c).wait_send()
            remote(
                staged.at[0, 0, part(c)], out.at[spot(mate, c)], mate_sem.at[c], out_recv.at[mate, c], rep=mate
            ).wait_recv()

    @pl.when(helps)
    def _():
        pan_pass.wait_send()
        code_pass.wait_send()
        for c in range(CHUNKS):
            for core in range(cores):
                back_out(core, c).wait_send()


def per_device(amplitudes, live_mask, integrals, coupled_tiles):
    count = lax.axis_size("virt")
    cores = lax.axis_size("rep")
    tiles, ks, width, _ = integrals.shape
    half = amplitudes.shape[0] // cores
    dma = pltpu.SemaphoreType.DMA
    kind = amplitudes.dtype
    return pl.pallas_call(
        ladder_kernel,
        out_shape=jax.ShapeDtypeStruct((amplitudes.shape[0], width), kind),
        in_specs=[
            pl.BlockSpec(memory_space=pl.ANY),
            pl.BlockSpec(memory_space=pltpu.SMEM),
            pl.BlockSpec(memory_space=pl.ANY),
            pl.BlockSpec(memory_space=pl.ANY),
        ],
        out_specs=pl.BlockSpec(memory_space=pl.ANY),
        scratch_shapes=[
            pltpu.VMEM((count, half, tiles * width), kind),
            pltpu.VMEM((2, cores, tiles, ks, width, width), kind),
            pltpu.VMEM((2, cores, tiles, ks), jnp.int32),
            pltpu.SMEM((2, cores, tiles, ks), jnp.int32),
            pltpu.VMEM((2, count, tiles * width, tiles * width), kind),
            pltpu.VMEM((2, tiles, half, width), kind),
            dma((CHUNKS,)),
            dma((count, CHUNKS)),
            dma((count, CHUNKS)),
            dma((count, CHUNKS)),
            dma(()),
            dma((3,)),
            dma((3,)),
            dma(()),
            dma((3,)),
            dma((3,)),
            dma(()),
            dma((CHUNKS,)),
            dma((CHUNKS,)),
            dma((cores, CHUNKS)),
            dma((cores, CHUNKS)),
        ],
        compiler_params=pltpu.CompilerParams(
            collective_id=0, has_side_effects=True, vmem_limit_bytes=48 * 1024 * 1024
        ),
    )(amplitudes, live_mask, integrals, coupled_tiles)


def solution(mesh):
    return jax.shard_map(
        per_device,
        mesh=mesh,
        in_specs=(
            P(("groups", "occ"), "virt"),
            P(("groups", "occ"), "virt"),
            P(("groups", "virt"), "rep", None, None),
            P(("groups", "virt"), "rep"),
        ),
        out_specs=P(("groups", "occ"), ("virt", "rep")),
        check_vma=False,
    )
```

```python
import functools

import jax
import jax.numpy as jnp
from jax import lax
from jax.experimental import pallas as pl
from jax.experimental.pallas import tpu as pltpu
from jax.sharding import PartitionSpec as P

MESH = pl.DeviceIdType.MESH
CHUNKS = 4


def ladder_kernel(
    amps, live_in, ints, pattern, out,
    live, held, panels, codes, codes_s, dense, staged,
    live_sem, load_sem, send_r, send_l, recv_sem,
    pan_load, pan_recv, pan_send, code_load, code_recv, code_send, code_copy,
    own_sem, mate_sem, back_sem, out_recv,
):
    count = lax.axis_size("virt")
    cores = lax.axis_size("rep")
    z = lax.axis_index("virt")
    r = lax.axis_index("rep")
    mate = 1 - r
    last = count - 1
    tiles, ks, width, _ = ints.shape
    half = held.shape[1]
    rows = half // CHUNKS
    block = amps.shape[0] // live.shape[1]
    is_end = jnp.logical_or(z == 0, z == last)
    works = jnp.logical_not(is_end)
    helps = jnp.logical_or(z == 1, z == last - 1)
    helper = jnp.where(z == 0, 1, last - 1)
    helped = jnp.where(z == 1, 0, last)

    barrier = pltpu.get_barrier_semaphore()
    pl.semaphore_signal(barrier, inc=1, device_id={"rep": mate}, device_id_type=MESH)

    @pl.when(z > 0)
    def _():
        for c in range(cores):
            pl.semaphore_signal(barrier, inc=1, device_id={"virt": z - 1, "rep": c}, device_id_type=MESH)

    @pl.when(z < last)
    def _():
        for c in range(cores):
            pl.semaphore_signal(barrier, inc=1, device_id={"virt": z + 1, "rep": c}, device_id_type=MESH)

    def part(c):
        return pl.ds(pl.multiple_of(c * rows, rows), rows)

    def load(c):
        start = pl.multiple_of(r * half + c * rows, rows)
        return pltpu.make_async_copy(amps.at[pl.ds(start, rows)], held.at[z, part(c)], load_sem.at[c])

    live_load = pltpu.make_async_copy(live_in, live, live_sem)
    live_load.start()
    lax.fori_loop(0, CHUNKS, lambda c, _: (load(c).start(), 0)[1], 0)
    pan_in = pltpu.make_async_copy(ints, panels.at[0, r], pan_load)
    code_in = pltpu.make_async_copy(pattern, codes.at[0, r], code_load)
    pan_in.start()
    code_in.start()

    def remote(src, dst, send, recv, **where):
        return pltpu.make_async_remote_copy(
            src_ref=src, dst_ref=dst, send_sem=send, recv_sem=recv, device_id=where, device_id_type=MESH
        )

    pan_mate = remote(panels.at[0, r], panels.at[0, r], pan_send.at[0], pan_recv.at[0], rep=mate)
    code_mate = remote(codes.at[0, r], codes.at[0, r], code_send.at[0], code_recv.at[0], rep=mate)
    pan_help = remote(panels.at[0, r], panels.at[1, r], pan_send.at[1], pan_recv.at[1], virt=helper)
    code_help = remote(codes.at[0, r], codes.at[1, r], code_send.at[1], code_recv.at[1], virt=helper)
    pan_pass = remote(panels.at[1, r], panels.at[1, r], pan_send.at[2], pan_recv.at[2], rep=mate)
    code_pass = remote(codes.at[1, r], codes.at[1, r], code_send.at[2], code_recv.at[2], rep=mate)

    def to_right(j, c):
        return remote(held.at[j, part(c)], held.at[j, part(c)], send_r.at[j, c], recv_sem.at[j, c], virt=z + 1)

    def to_left(j, c):
        return remote(held.at[j, part(c)], held.at[j, part(c)], send_l.at[j, c], recv_sem.at[j, c], virt=z - 1)

    goes_right = z + 1 <= last - 1
    goes_left = z - 1 >= 1


    def mask(c):
        def one(b, _):
            at = pl.multiple_of(c * rows + b * block, block)
            which = (r * half + c * rows) // block + b
            for t in range(tiles):
                keep = live[t, which].astype(jnp.float32)
                keep = jnp.full((block, width), keep, jnp.float32).astype(held.dtype)
                view = held.at[z, pl.ds(at, block), pl.ds(t * width, width)]
                view[...] = view[...] * keep
            return 0

        lax.fori_loop(0, rows // block, one, 0, unroll=rows // block <= 8)

    live_load.wait()
    load(0).wait()
    mask(0)
    pl.semaphore_wait(barrier, 1 + cores * ((z > 0).astype(jnp.int32) + (z < last).astype(jnp.int32)))

    pan_in.wait()
    code_in.wait()

    @pl.when(is_end)
    def _():
        pan_help.start()
        code_help.start()

    def launch(c, _):
        @pl.when(c > 0)
        def _():
            load(c).wait()
            mask(c)

        @pl.when(goes_right)
        def _():
            to_right(z, c).start()

        @pl.when(goes_left)
        def _():
            to_left(z, c).start()

        return 0

    @pl.when(works)
    def _():
        pan_mate.start()
        code_mate.start()

    lax.fori_loop(0, CHUNKS, launch, 0)

    def build(g):
        copy = pltpu.make_async_copy(codes.at[g], codes_s.at[g], code_copy)
        copy.start()
        copy.wait()

        def one(j, _):
            for t in range(tiles):
                for i in range(tiles):
                    total = jnp.zeros((width, width), dense.dtype)
                    for c in range(cores):
                        for k in range(ks):
                            hit = (codes_s[g, c, i, k] == j * tiles + t).astype(jnp.float32)
                            hit = jnp.full((width, width), hit, jnp.float32).astype(dense.dtype)
                            total = total + hit * panels[g, c, i, k]
                    dense[g, j, pl.ds(t * width, width), pl.ds(i * width, width)] = total
            return 0

        lax.fori_loop(0, count, one, 0)

    def arrive(j, c):
        to_right(j, c).wait_recv()

    def forward(c):
        def one(d, _):
            left, right = z - d, z + d

            @pl.when(jnp.logical_and(left >= 0, goes_right))
            def _():
                arrive(left, c)
                to_right(left, c).start()

            @pl.when(jnp.logical_and(right <= last, goes_left))
            def _():
                arrive(right, c)
                to_left(right, c).start()

            return 0

        lax.fori_loop(1, count, one, 0)

    def settle(c):
        def one(d, _):
            left, right = z - d, z + d

            @pl.when(jnp.logical_and(left >= 0, jnp.logical_not(goes_right)))
            def _():
                arrive(left, c)

            @pl.when(jnp.logical_and(right <= last, jnp.logical_not(goes_left)))
            def _():
                arrive(right, c)

            return 0

        lax.fori_loop(1, count, one, 0)

    def spot(owner, c):
        return pl.ds(pl.multiple_of(owner * half + c * rows, rows), rows)

    def own_out(c):
        return pltpu.make_async_copy(staged.at[0, r, part(c)], out.at[spot(r, c)], own_sem.at[c])

    def mate_out(c):
        return remote(
            staged.at[0, mate, part(c)], out.at[spot(r, c)], mate_sem.at[c], out_recv.at[r, c], rep=mate
        )

    def back_out(core, c):
        return remote(
            staged.at[1, core, part(c)], out.at[spot(r, c)], back_sem.at[core, c], out_recv.at[r, c],
            virt=helped, rep=core,
        )

    step = min(rows, 128)

    def multiply(g, c):
        def one(s, _):
            at = pl.ds(pl.multiple_of(c * rows + s * step, step), step)
            total = jnp.zeros((step, tiles * width), jnp.float32)
            for j in range(count):
                total = total + jnp.dot(held[j, at], dense[g, j], preferred_element_type=jnp.float32)
            for i in range(tiles):
                staged[g, i, at] = total[:, i * width : (i + 1) * width].astype(staged.dtype)
            return 0

        lax.fori_loop(0, rows // step, one, 0)

    @pl.when(works)
    def _():
        pan_mate.wait_recv()
        code_mate.wait_recv()
        build(0)

    @pl.when(helps)
    def _():
        pan_help.wait_recv()
        code_help.wait_recv()
        pan_pass.start()
        code_pass.start()

    @pl.when(works)
    def _():
        forward(0)

    @pl.when(helps)
    def _():
        pan_pass.wait_recv()
        code_pass.wait_recv()
        build(1)

    def finish(c, _):
        @pl.when(c + 1 < CHUNKS)
        def _():
            forward(c + 1)

        settle(c)

        @pl.when(helps)
        def _():
            multiply(1, c)
            for core in range(cores):
                back_out(core, c).start()

        multiply(0, c)
        mate_out(c).start()
        own_out(c).start()
        return 0

    @pl.when(works)
    def _():
        lax.fori_loop(0, CHUNKS, finish, 0)

    @pl.when(is_end)
    def _():
        pan_help.wait_send()
        code_help.wait_send()

        def collect(c, _):
            for core in range(cores):
                remote(
                    staged.at[0, 0, part(c)], out.at[spot(core, c)], mate_sem.at[c], out_recv.at[core, c], rep=mate
                ).wait_recv()
            return 0

        lax.fori_loop(0, CHUNKS, collect, 0)

    def drain(c, _):
        @pl.when(goes_right)
        def _():
            to_right(z, c).wait_send()

        @pl.when(goes_left)
        def _():
            to_left(z, c).wait_send()

        @pl.when(works)
        def _():
            def one(d, _):
                left, right = z - d, z + d

                @pl.when(jnp.logical_and(left >= 0, goes_right))
                def _():
                    to_right(left, c).wait_send()

                @pl.when(jnp.logical_and(right <= last, goes_left))
                def _():
                    to_left(right, c).wait_send()

                return 0

            lax.fori_loop(1, count, one, 0)
            own_out(c).wait()
            mate_out(c).wait_send()
            remote(
                staged.at[0, 0, part(c)], out.at[spot(mate, c)], mate_sem.at[c], out_recv.at[mate, c], rep=mate
            ).wait_recv()

        @pl.when(helps)
        def _():
            for core in range(cores):
                back_out(core, c).wait_send()

        return 0

    lax.fori_loop(0, CHUNKS, drain, 0)

    @pl.when(works)
    def _():
        pan_mate.wait_send()
        code_mate.wait_send()

    @pl.when(helps)
    def _():
        pan_pass.wait_send()
        code_pass.wait_send()


def per_device(amplitudes, live_mask, integrals, coupled_tiles):
    count = lax.axis_size("virt")
    cores = lax.axis_size("rep")
    tiles, ks, width, _ = integrals.shape
    half = amplitudes.shape[0] // cores
    dma = pltpu.SemaphoreType.DMA
    kind = amplitudes.dtype
    return pl.pallas_call(
        ladder_kernel,
        out_shape=jax.ShapeDtypeStruct((amplitudes.shape[0], width), kind),
        in_specs=[
            pl.BlockSpec(memory_space=pltpu.HBM),
            pl.BlockSpec(memory_space=pltpu.HBM),
            pl.BlockSpec(memory_space=pltpu.HBM),
            pl.BlockSpec(memory_space=pltpu.HBM),
        ],
        out_specs=pl.BlockSpec(memory_space=pl.ANY),
        scratch_shapes=[
            pltpu.SMEM(live_mask.shape[::-1], jnp.int32),
            pltpu.VMEM((count, half, tiles * width), kind),
            pltpu.VMEM((2, cores, tiles, ks, width, width), kind),
            pltpu.VMEM((2, cores, tiles, ks), jnp.int32),
            pltpu.SMEM((2, cores, tiles, ks), jnp.int32),
            pltpu.VMEM((2, count, tiles * width, tiles * width), kind),
            pltpu.VMEM((2, tiles, half, width), kind),
            dma(()),
            dma((CHUNKS,)),
            dma((count, CHUNKS)),
            dma((count, CHUNKS)),
            dma((count, CHUNKS)),
            dma(()),
            dma((3,)),
            dma((3,)),
            dma(()),
            dma((3,)),
            dma((3,)),
            dma(()),
            dma((CHUNKS,)),
            dma((CHUNKS,)),
            dma((cores, CHUNKS)),
            dma((cores, CHUNKS)),
        ],
        compiler_params=pltpu.CompilerParams(
            collective_id=0, has_side_effects=True, vmem_limit_bytes=48 * 1024 * 1024
        ),
    )(*[pltpu.with_memory_space_constraint(x, pltpu.HBM) for x in (amplitudes, live_mask.T, integrals, coupled_tiles)])


def solution(mesh):
    return jax.shard_map(
        per_device,
        mesh=mesh,
        in_specs=(
            P(("groups", "occ"), "virt"),
            P(("groups", "occ"), "virt"),
            P(("groups", "virt"), "rep", None, None),
            P(("groups", "virt"), "rep"),
        ),
        out_specs=P(("groups", "occ"), ("virt", "rep")),
        check_vma=False,
    )
```

```python
import functools

import jax
import jax.numpy as jnp
from jax import lax
from jax.experimental import pallas as pl
from jax.experimental.pallas import tpu as pltpu
from jax.sharding import PartitionSpec as P

MESH = pl.DeviceIdType.MESH
CHUNKS = 4


def ladder_kernel(
    amps, live_in, ints, pattern, out,
    live, held, panels, codes, codes_s, dense, staged,
    live_sem, load_sem, send_r, send_l, recv_sem,
    pan_load, pan_recv, pan_send, code_load, code_recv, code_send, code_copy,
    own_sem, mate_sem, back_sem, out_recv,
):
    count = lax.axis_size("virt")
    cores = lax.axis_size("rep")
    z = lax.axis_index("virt")
    r = lax.axis_index("rep")
    mate = 1 - r
    last = count - 1
    tiles, ks, width, _ = ints.shape
    half = held.shape[1]
    rows = half // CHUNKS
    block = amps.shape[0] // live.shape[1]
    is_end = jnp.logical_or(z == 0, z == last)
    works = jnp.logical_not(is_end)
    helps = jnp.logical_or(z == 1, z == last - 1)
    helper = jnp.where(z == 0, 1, last - 1)
    helped = jnp.where(z == 1, 0, last)

    barrier = pltpu.get_barrier_semaphore()
    pl.semaphore_signal(barrier, inc=1, device_id={"rep": mate}, device_id_type=MESH)

    @pl.when(z > 0)
    def _():
        for c in range(cores):
            pl.semaphore_signal(barrier, inc=1, device_id={"virt": z - 1, "rep": c}, device_id_type=MESH)

    @pl.when(z < last)
    def _():
        for c in range(cores):
            pl.semaphore_signal(barrier, inc=1, device_id={"virt": z + 1, "rep": c}, device_id_type=MESH)

    def part(c):
        return pl.ds(pl.multiple_of(c * rows, rows), rows)

    def load(c):
        start = pl.multiple_of(r * half + c * rows, rows)
        return pltpu.make_async_copy(amps.at[pl.ds(start, rows)], held.at[z, part(c)], load_sem.at[c])

    live_load = pltpu.make_async_copy(live_in, live, live_sem)
    live_load.start()
    lax.fori_loop(0, CHUNKS, lambda c, _: (load(c).start(), 0)[1], 0)
    pan_in = pltpu.make_async_copy(ints, panels.at[0, r], pan_load)
    code_in = pltpu.make_async_copy(pattern, codes.at[0, r], code_load)
    pan_in.start()
    code_in.start()

    def remote(src, dst, send, recv, **where):
        return pltpu.make_async_remote_copy(
            src_ref=src, dst_ref=dst, send_sem=send, recv_sem=recv, device_id=where, device_id_type=MESH
        )

    pan_mate = remote(panels.at[0, r], panels.at[0, r], pan_send.at[0], pan_recv.at[0], rep=mate)
    code_mate = remote(codes.at[0, r], codes.at[0, r], code_send.at[0], code_recv.at[0], rep=mate)
    pan_help = remote(panels.at[0, r], panels.at[1, r], pan_send.at[1], pan_recv.at[1], virt=helper)
    code_help = remote(codes.at[0, r], codes.at[1, r], code_send.at[1], code_recv.at[1], virt=helper)
    pan_pass = remote(panels.at[1, r], panels.at[1, r], pan_send.at[2], pan_recv.at[2], rep=mate)
    code_pass = remote(codes.at[1, r], codes.at[1, r], code_send.at[2], code_recv.at[2], rep=mate)

    def to_right(j, c):
        return remote(held.at[j, part(c)], held.at[j, part(c)], send_r.at[j, c], recv_sem.at[j, c], virt=z + 1)

    def to_left(j, c):
        return remote(held.at[j, part(c)], held.at[j, part(c)], send_l.at[j, c], recv_sem.at[j, c], virt=z - 1)

    goes_right = z + 1 <= last - 1
    goes_left = z - 1 >= 1


    def mask(c):
        def one(b, _):
            at = pl.multiple_of(c * rows + b * block, block)
            which = (r * half + c * rows) // block + b
            for t in range(tiles):
                keep = live[t, which].astype(jnp.float32)
                keep = jnp.full((block, width), keep, jnp.float32).astype(held.dtype)
                view = held.at[z, pl.ds(at, block), pl.ds(t * width, width)]
                view[...] = view[...] * keep
            return 0

        lax.fori_loop(0, rows // block, one, 0, unroll=rows // block <= 8)

    live_load.wait()
    load(0).wait()
    mask(0)
    pl.semaphore_wait(barrier, 1 + cores * ((z > 0).astype(jnp.int32) + (z < last).astype(jnp.int32)))

    pan_in.wait()
    code_in.wait()

    @pl.when(is_end)
    def _():
        pan_help.start()
        code_help.start()
        pan_help.wait_send()
        code_help.wait_send()

    def launch(c, _):
        @pl.when(c > 0)
        def _():
            load(c).wait()
            mask(c)

        @pl.when(goes_right)
        def _():
            to_right(z, c).start()

        @pl.when(goes_left)
        def _():
            to_left(z, c).start()

        return 0

    @pl.when(works)
    def _():
        pan_mate.start()
        code_mate.start()

    lax.fori_loop(0, CHUNKS, launch, 0)

    def build(g):
        copy = pltpu.make_async_copy(codes.at[g], codes_s.at[g], code_copy)
        copy.start()
        copy.wait()

        def one(j, _):
            for t in range(tiles):
                for i in range(tiles):
                    total = jnp.zeros((width, width), dense.dtype)
                    for c in range(cores):
                        for k in range(ks):
                            hit = (codes_s[g, c, i, k] == j * tiles + t).astype(jnp.float32)
                            hit = jnp.full((width, width), hit, jnp.float32).astype(dense.dtype)
                            total = total + hit * panels[g, c, i, k]
                    dense[g, j, pl.ds(t * width, width), pl.ds(i * width, width)] = total
            return 0

        lax.fori_loop(0, count, one, 0)

    def arrive(j, c):
        to_right(j, c).wait_recv()

    def forward(c, _):
        def one(d, _):
            left, right = z - d, z + d

            @pl.when(jnp.logical_and(left >= 0, goes_right))
            def _():
                arrive(left, c)
                to_right(left, c).start()

            @pl.when(jnp.logical_and(right <= last, goes_left))
            def _():
                arrive(right, c)
                to_left(right, c).start()

            return 0

        lax.fori_loop(1, count, one, 0)
        return 0

    def settle(c):
        def one(d, _):
            left, right = z - d, z + d

            @pl.when(jnp.logical_and(left >= 0, jnp.logical_not(goes_right)))
            def _():
                arrive(left, c)

            @pl.when(jnp.logical_and(right <= last, jnp.logical_not(goes_left)))
            def _():
                arrive(right, c)

            return 0

        lax.fori_loop(1, count, one, 0)

    def spot(owner, c):
        return pl.ds(pl.multiple_of(owner * half + c * rows, rows), rows)

    def own_out(c):
        return pltpu.make_async_copy(staged.at[0, r, part(c)], out.at[spot(r, c)], own_sem.at[c])

    def mate_out(c):
        return remote(
            staged.at[0, mate, part(c)], out.at[spot(r, c)], mate_sem.at[c], out_recv.at[r, c], rep=mate
        )

    def back_out(core, c):
        return remote(
            staged.at[1, core, part(c)], out.at[spot(r, c)], back_sem.at[core, c], out_recv.at[r, c],
            virt=helped, rep=core,
        )

    step = min(rows, 128)

    def multiply(g, c):
        def one(s, _):
            at = pl.ds(pl.multiple_of(c * rows + s * step, step), step)
            total = jnp.zeros((step, tiles * width), jnp.float32)
            for j in range(count):
                total = total + jnp.dot(held[j, at], dense[g, j], preferred_element_type=jnp.float32)
            for i in range(tiles):
                staged[g, i, at] = total[:, i * width : (i + 1) * width].astype(staged.dtype)
            return 0

        lax.fori_loop(0, rows // step, one, 0)

    @pl.when(helps)
    def _():
        pan_help.wait_recv()
        code_help.wait_recv()
        pan_pass.start()
        code_pass.start()

    @pl.when(works)
    def _():
        pan_mate.wait_recv()
        code_mate.wait_recv()
        build(0)

    @pl.when(works)
    def _():
        lax.fori_loop(0, CHUNKS, forward, 0)

    @pl.when(helps)
    def _():
        pan_pass.wait_recv()
        code_pass.wait_recv()
        build(1)

    def finish(c, _):
        settle(c)

        @pl.when(helps)
        def _():
            multiply(1, c)
            for core in range(cores):
                back_out(core, c).start()

        multiply(0, c)
        mate_out(c).start()
        own_out(c).start()
        return 0

    @pl.when(works)
    def _():
        lax.fori_loop(0, CHUNKS, finish, 0)

    @pl.when(is_end)
    def _():
        def collect(c, _):
            for core in range(cores):
                remote(
                    staged.at[0, 0, part(c)], out.at[spot(core, c)], mate_sem.at[c], out_recv.at[core, c], rep=mate
                ).wait_recv()
            return 0

        lax.fori_loop(0, CHUNKS, collect, 0)

    def drain(c, _):
        @pl.when(goes_right)
        def _():
            to_right(z, c).wait_send()

        @pl.when(goes_left)
        def _():
            to_left(z, c).wait_send()

        @pl.when(works)
        def _():
            def one(d, _):
                left, right = z - d, z + d

                @pl.when(jnp.logical_and(left >= 0, goes_right))
                def _():
                    to_right(left, c).wait_send()

                @pl.when(jnp.logical_and(right <= last, goes_left))
                def _():
                    to_left(right, c).wait_send()

                return 0

            lax.fori_loop(1, count, one, 0)
            own_out(c).wait()
            mate_out(c).wait_send()
            remote(
                staged.at[0, 0, part(c)], out.at[spot(mate, c)], mate_sem.at[c], out_recv.at[mate, c], rep=mate
            ).wait_recv()

        @pl.when(helps)
        def _():
            for core in range(cores):
                back_out(core, c).wait_send()

        return 0

    lax.fori_loop(0, CHUNKS, drain, 0)

    @pl.when(works)
    def _():
        pan_mate.wait_send()
        code_mate.wait_send()

    @pl.when(helps)
    def _():
        pan_pass.wait_send()
        code_pass.wait_send()


def per_device(amplitudes, live_mask, integrals, coupled_tiles):
    count = lax.axis_size("virt")
    cores = lax.axis_size("rep")
    tiles, ks, width, _ = integrals.shape
    half = amplitudes.shape[0] // cores
    dma = pltpu.SemaphoreType.DMA
    kind = amplitudes.dtype
    return pl.pallas_call(
        ladder_kernel,
        out_shape=jax.ShapeDtypeStruct((amplitudes.shape[0], width), kind),
        in_specs=[
            pl.BlockSpec(memory_space=pltpu.HBM),
            pl.BlockSpec(memory_space=pltpu.HBM),
            pl.BlockSpec(memory_space=pltpu.HBM),
            pl.BlockSpec(memory_space=pltpu.HBM),
        ],
        out_specs=pl.BlockSpec(memory_space=pl.ANY),
        scratch_shapes=[
            pltpu.SMEM(live_mask.shape[::-1], jnp.int32),
            pltpu.VMEM((count, half, tiles * width), kind),
            pltpu.VMEM((2, cores, tiles, ks, width, width), kind),
            pltpu.VMEM((2, cores, tiles, ks), jnp.int32),
            pltpu.SMEM((2, cores, tiles, ks), jnp.int32),
            pltpu.VMEM((2, count, tiles * width, tiles * width), kind),
            pltpu.VMEM((2, tiles, half, width), kind),
            dma(()),
            dma((CHUNKS,)),
            dma((count, CHUNKS)),
            dma((count, CHUNKS)),
            dma((count, CHUNKS)),
            dma(()),
            dma((3,)),
            dma((3,)),
            dma(()),
            dma((3,)),
            dma((3,)),
            dma(()),
            dma((CHUNKS,)),
            dma((CHUNKS,)),
            dma((cores, CHUNKS)),
            dma((cores, CHUNKS)),
        ],
        compiler_params=pltpu.CompilerParams(
            collective_id=0, has_side_effects=True, vmem_limit_bytes=48 * 1024 * 1024
        ),
    )(*[pltpu.with_memory_space_constraint(x, pltpu.HBM) for x in (amplitudes, live_mask.T, integrals, coupled_tiles)])


def solution(mesh):
    return jax.shard_map(
        per_device,
        mesh=mesh,
        in_specs=(
            P(("groups", "occ"), "virt"),
            P(("groups", "occ"), "virt"),
            P(("groups", "virt"), "rep", None, None),
            P(("groups", "virt"), "rep"),
        ),
        out_specs=P(("groups", "occ"), ("virt", "rep")),
        check_vma=False,
    )
```
